32 devices in a mesh: seq: 8 (over z, y), exp: 4 (over x, core).
Axes of the slice: x: 2, y: 2, z: 4, core: 2. Of those that a mesh axis runs over, the one named last changes fastest.
Arguments:
- queries: bfloat16 [2048, 6144], P('seq', 'exp'), may hold values from -6 to 6
- key_rows: bfloat16 [2048, 6144], P('seq', 'exp'), may hold values from -6 to 6
- value_rows: bfloat16 [2048, 6144], P('seq', 'exp'), may hold values from -6 to 6
- log_decay: float32 [2048, 48], P('seq', 'exp'), may hold values from -1 to 0, as said below
- residual: bfloat16 [2048, 6144], P('seq', 'exp'), may hold values from -6 to 6
- head_gain: float32 [6144], P('exp'), may hold values from 0.1 to 1.9
- moe_gain: float32 [6144], replicated, may hold values from 0.1 to 1.9
- routes: int32 [2048, 2], P(('seq', 'exp')), may hold values from 0 to 7, all different within a row; in each aligned block of 64 rows (0 to 63, 64 to 127, ...) at most 20 rows name the same one
- route_weight: float32 [2048, 2], P(('seq', 'exp')), may hold values from 0.2 to 1
- up_weight: bfloat16 [8, 6144, 9216], P('exp', None, 'seq'), may hold values from -0.078125 to 0.078125
- down_weight: bfloat16 [8, 9216, 6144], P('exp', 'seq'), may hold values from -0.0625 to 0.0625
Outputs:
- layer_out: bfloat16 [2048, 6144], P(('seq', 'exp'))
The draws below stay inside these ranges and needn't reach their ends.
Inputs may be any that keep to these rules, and one draw needn't show every extreme that they name: `log_decay`: every entry is negative. `routes`: A row names two different experts. In each aligned block of 64 rows no expert is named more than 20 times, a bound that some block reaches.
All inputs are finite; a program needn't handle non-finite values.
Results may differ from the reference program's by a relative error of at most 0.012.
Values may be sent and summed in bfloat16 or wider, within the bound.
A program may use at most 192 MiB of HBM per device.

```python
import math
import jax
import jax.numpy as jnp
import numpy as np
from jax import lax

HEAD_TOTAL = 48
HEAD_DIM = 128
D = 6144
BLK = 256
TOK_DEV = 256
TOKEN_TOTAL = 2048
EXPERTS = 8
EXP_HID = 9216
ROWS_DEV = 64
CAP = 20
N_SEQ = 8


def draw_log_decay(key, part):
    key = jax.random.fold_in(key, 7)
    random_subkeys = jax.random.split(key, 7)
    fast_share = 0.5
    fast_heads = jax.random.bernoulli(random_subkeys[0], fast_share, (HEAD_TOTAL,))
    fast_rate = jnp.exp(jax.random.uniform(random_subkeys[1], (HEAD_TOTAL,), jnp.float32, math.log(1.0 / 50.0), math.log(1.0 / 30.0)))
    slow_rate = jnp.exp(jax.random.uniform(random_subkeys[2], (HEAD_TOTAL,), jnp.float32, math.log(0.05), math.log(0.3))) * (math.log(10.0) / TOKEN_TOTAL)
    baseline_decay_rate = jnp.where(fast_heads, fast_rate, slow_rate)
    per_device_scale = jnp.exp(jax.random.uniform(random_subkeys[3], (TOKEN_TOTAL // TOK_DEV, HEAD_TOTAL), jnp.float32, math.log(0.5), math.log(2.0)))
    per_device_scale = jnp.repeat(per_device_scale, TOK_DEV, axis=0)
    random_noise = jax.random.uniform(random_subkeys[4], (TOKEN_TOTAL, HEAD_TOTAL), jnp.float32, 0.5, 2.0)
    spike_locations = jax.random.randint(random_subkeys[5], (2,), 0, TOKEN_TOTAL)
    spike_mask = jnp.any(jnp.arange(TOKEN_TOTAL)[:, None] == spike_locations[None, :], axis=1).astype(jnp.float32)
    spike_loss = -jnp.log(jax.random.uniform(random_subkeys[6], (TOKEN_TOTAL, HEAD_TOTAL), jnp.float32, 0.6, 0.8))
    return -(baseline_decay_rate[None, :] * per_device_scale * random_noise + spike_mask[:, None] * spike_loss)


def level_of(own_key, dims, cuts, smallest, high):
    factor_of = 1.0
    for position, blocks in cuts:
        steps = jax.random.uniform(jax.random.fold_in(jax.random.fold_in(own_key, 6), position), (blocks,), jnp.float32, smallest / len(cuts), high / len(cuts))
        factor_of = factor_of * jnp.repeat(jnp.exp(steps), dims[position] // blocks).reshape((-1,) + (1,) * (len(dims) - 1 - position))
    return factor_of


def deal_out(stream_key, own, number, rows, count, top, most, lean):
    sequence = jax.random.permutation(stream_key, count)
    crowded, common = load_shares(count, rows * top, most, lean, True), load_shares(count, rows * top, most, lean, False)
    places = jnp.arange(count)

    def named(lengths, turn):
        used = int((lengths > 0).sum())
        fixed = max(1, used // 4)
        moved = fixed + (places - fixed + turn * (used - fixed)) % max(1, count - fixed)
        return jnp.zeros((count,), jnp.int32).at[sequence[jnp.where(places < fixed, places, moved)]].set(jnp.asarray(lengths, jnp.int32))

    lengths = jnp.where(number % 4 == 0, named(crowded, number // 4), named(common, number - number // 4 - 1))
    mixed = jax.random.permutation(jax.random.fold_in(own, 3), count)
    donor, receiver = mixed[0:count // 2 * 2:2], mixed[1:count // 2 * 2:2]
    room = jnp.minimum(lengths[donor] - 1, most - lengths[receiver]) // 2
    room = jnp.where((donor == sequence[0]) | (receiver == sequence[0]) | (lengths[receiver] == 0), 0, jnp.maximum(room, 0))
    moved = jax.random.randint(jax.random.fold_in(own, 4), (count // 2,), 0, 1 << 20) % (room + 1)
    lengths = lengths.at[donor].add(-moved).at[receiver].add(moved)
    members = jnp.searchsorted(jnp.cumsum(lengths), jnp.arange(rows * top), side="right").astype(jnp.int32)
    grid = members.reshape(top, rows).T
    grid = grid[jax.random.permutation(jax.random.fold_in(own, 1), rows)]
    turn = jax.random.randint(jax.random.fold_in(own, 2), (rows, 1), 0, top)
    return jnp.take_along_axis(grid, (jnp.arange(top)[None, :] + turn) % top, axis=1)


def load_shares(number_of, total, limit, skew, full):
    weights = [(1 << 20) // math.isqrt(rank ** skew) + 1 for rank in range(1, number_of + 1)]
    largest = limit if full else min(limit, max(-(-total // number_of), total * weights[0] // sum(weights)))
    least = 1 if total - largest >= number_of - 1 else 0
    counts, rest = [largest] + [least] * (number_of - 1), total - largest - least * (number_of - 1)
    while rest > 0:
        movable = [i for i in range(1, number_of) if counts[i] < largest] or [i for i in range(1, number_of) if counts[i] < limit]
        pool, left = sum([weights[i] for i in movable]), rest
        for i in movable:
            more = min(limit - counts[i], max(1, left * weights[i] // pool), rest)
            counts[i] = counts[i] + more
            rest = rest - more
    return np.array(counts)


def centred(stream_key, shape, deviation, reach, cuts=(), held_as=jnp.bfloat16):
    loudness = level_of(stream_key, shape, cuts, -0.22, 0.18) if cuts else 1.0
    result = jax.random.normal(stream_key, shape, jnp.float32) * deviation * loudness
    return jnp.minimum(jnp.maximum(result, -reach), reach).astype(held_as)


def setup_inputs(seed: int = 0) -> dict:
    key_of = jax.random.split(jax.random.key(seed), 12)
    queries = centred(key_of[0], (TOKEN_TOTAL, D), 1.0, 6.0, ((0, 8), (1, 4)))
    key_rows = centred(key_of[1], (TOKEN_TOTAL, D), 1.0, 6.0, ((0, 8), (1, 4)))
    value_rows = centred(key_of[2], (TOKEN_TOTAL, D), 1.0, 6.0, ((0, 8), (1, 4)))
    log_decay = draw_log_decay(jax.random.fold_in(key_of[11], 71), 0)
    residual = centred(key_of[4], (TOKEN_TOTAL, D), 1.0, 6.0, ((0, 8), (1, 4)))
    head_gain = jnp.clip(1.0 + 0.18 * jax.random.normal(key_of[5], (D,), jnp.float32), 0.1, 1.9)
    moe_gain = jnp.clip(1.0 + 0.18 * jax.random.normal(key_of[6], (D,), jnp.float32), 0.1, 1.9)
    routes_keys = jax.random.split(jax.random.fold_in(key_of[7], 1), TOKEN_TOTAL // ROWS_DEV)
    routes_turns = jax.random.permutation(jax.random.fold_in(key_of[7], 3), TOKEN_TOTAL // ROWS_DEV)
    routes = jax.vmap(lambda own, number: deal_out(jax.random.fold_in(key_of[7], 2), own, number, ROWS_DEV, EXPERTS, 2, CAP, 2))(routes_keys, routes_turns).reshape((TOKEN_TOTAL, 2))
    route_weight = jnp.clip(0.2 + 0.8 * jax.random.uniform(key_of[8], (TOKEN_TOTAL, 2), jnp.float32) ** level_of(key_of[8], (TOKEN_TOTAL, 2), ((0, 32),), -0.2, 0.2), 0.2, 1.0)
    up_weight = centred(key_of[9], (EXPERTS, D, EXP_HID), D ** -0.5, 0.078125, ((0, 4), (2, 8)))
    down_weight = centred(key_of[10], (EXPERTS, EXP_HID, D), EXP_HID ** -0.5, 0.0625, ((0, 4), (1, 8)))
    return {"queries": queries, "key_rows": key_rows, "value_rows": value_rows, "log_decay": log_decay, "residual": residual, "head_gain": head_gain, "moe_gain": moe_gain, "routes": routes, "route_weight": route_weight, "up_weight": up_weight, "down_weight": down_weight}


def rounded(values):
    return lax.optimization_barrier(values.astype(jnp.bfloat16)).astype(jnp.float32)

def block_step(carry_state, blocks_in):
    query_blk, key_blk, value_blk, decay_blk = blocks_in
    cumulative = jnp.cumsum(decay_blk, axis=0)
    block_total = cumulative[-1]
    scores = jnp.einsum('thd,jhd->htj', query_blk.astype(jnp.float32), key_blk.astype(jnp.float32), precision=lax.Precision.HIGHEST)
    levels = jnp.transpose(cumulative)
    spread = levels[:, :, None] - levels[:, None, :]
    causal = jnp.tril(jnp.ones((BLK, BLK), dtype=bool))[None]
    weights = rounded(jnp.where(causal, jnp.exp(jnp.where(causal, spread, 0.0)), 0.0) * scores)
    inner_part = jnp.einsum('htj,jhd->thd', weights, value_blk.astype(jnp.float32), precision=lax.Precision.HIGHEST)
    query_faded = jnp.exp(cumulative)[:, :, None] * query_blk.astype(jnp.float32)
    carried_part = jnp.einsum('thd,hde->the', query_faded, carry_state, precision=lax.Precision.HIGHEST)
    key_faded = rounded(jnp.exp(block_total[None, :] - cumulative)[:, :, None] * key_blk.astype(jnp.float32))
    next_state = jnp.exp(block_total)[:, None, None] * carry_state + jnp.einsum('jhd,jhe->hde', key_faded, value_blk.astype(jnp.float32), precision=lax.Precision.HIGHEST)
    return (next_state, carried_part + inner_part)

def reference(queries, key_rows, value_rows, log_decay, residual, head_gain, moe_gain, routes, route_weight, up_weight, down_weight):
    block_count = TOKEN_TOTAL // BLK
    shaped = (block_count, BLK, HEAD_TOTAL, HEAD_DIM)
    blocks_in = (queries.reshape(shaped), key_rows.reshape(shaped), value_rows.reshape(shaped), log_decay.reshape(block_count, BLK, HEAD_TOTAL))
    start_state = jnp.zeros((HEAD_TOTAL, HEAD_DIM, HEAD_DIM), jnp.float32)
    ignored, attention = lax.scan(block_step, start_state, blocks_in)
    attention = attention.reshape(TOKEN_TOTAL, HEAD_TOTAL, HEAD_DIM)
    mean_square = lax.optimization_barrier(jnp.mean(attention * attention, axis=-1, keepdims=True))
    normed = attention * lax.rsqrt(mean_square + 1e-06) * head_gain.reshape(HEAD_TOTAL, HEAD_DIM)
    mixed_rows = (residual.astype(jnp.float32) + normed.reshape(TOKEN_TOTAL, D)).astype(jnp.bfloat16)
    mixed_float = mixed_rows.astype(jnp.float32)
    row_square = lax.optimization_barrier(jnp.mean(mixed_float * mixed_float, axis=-1, keepdims=True))
    norm_rows = (mixed_float * lax.rsqrt(row_square + 1e-06) * moe_gain).astype(jnp.bfloat16)
    pieces = N_SEQ
    piece_width = EXP_HID // pieces
    max_rows = TOKEN_TOTAL // ROWS_DEV * CAP
    flat_ids = routes.reshape(-1)
    padded_rows = jnp.concatenate([norm_rows, jnp.zeros((1, D), jnp.bfloat16)], axis=0)
    padded_weight = jnp.concatenate([route_weight.reshape(-1), jnp.zeros((1,), jnp.float32)], axis=0)

    def per_expert(accumulated, expert):
        pair_index = jnp.nonzero(flat_ids == expert, size=max_rows, fill_value=2 * TOKEN_TOTAL)[0].astype(jnp.int32)
        token_index = pair_index // 2
        picked = padded_rows[token_index]
        up_piece = up_weight[expert]
        down_piece = down_weight[expert]
        activated = jax.nn.silu(jnp.dot(picked, up_piece, preferred_element_type=jnp.float32)).astype(jnp.bfloat16)
        expert_out = jnp.zeros((max_rows, D), jnp.float32)
        for piece in range(pieces):
            lo_col = piece * piece_width
            term = jnp.dot(activated[:, lo_col:lo_col + piece_width], down_piece[lo_col:lo_col + piece_width], preferred_element_type=jnp.float32)
            expert_out = expert_out + rounded(term)
        contribution = expert_out * padded_weight[pair_index][:, None]
        accumulated = accumulated.at[token_index].add(contribution, mode='drop')
        return (accumulated, None)
    accumulated, ignored_too = lax.scan(per_expert, jnp.zeros((TOKEN_TOTAL, D), jnp.float32), jnp.arange(EXPERTS, dtype=jnp.int32))
    return (mixed_float + accumulated).astype(jnp.bfloat16)
```

```python
import jax
import jax.numpy as jnp
from jax import lax
from jax.sharding import PartitionSpec as P

HEAD_DIM = 128
BLK = 256
EXPERTS = 8


def expert_part(rows, up_weight, down_weight):
    hidden = jax.nn.silu(jnp.dot(rows, up_weight, preferred_element_type=jnp.float32)).astype(
        jnp.bfloat16
    )
    return jnp.dot(hidden, down_weight, preferred_element_type=jnp.float32).astype(jnp.bfloat16)


def per_device(
    queries,
    key_rows,
    value_rows,
    log_decay,
    residual,
    head_gain,
    moe_gain,
    routes,
    route_weight,
    up_weight,
    down_weight,
):
    token_count, feature_dim = queries.shape
    head_count = log_decay.shape[1]
    block_count = token_count // BLK
    shaped = (block_count, BLK, head_count, HEAD_DIM)
    query_blk = queries.reshape(shaped)
    key_blk = key_rows.reshape(shaped)
    value_blk = value_rows.reshape(shaped)
    cumulative = jnp.cumsum(log_decay.reshape(block_count, BLK, head_count), axis=1)
    totals = cumulative[:, -1, :]
    scores = jnp.einsum("bthd,bjhd->bhtj", query_blk, key_blk, preferred_element_type=jnp.float32)
    levels = jnp.transpose(cumulative, (0, 2, 1))
    spread = levels[:, :, :, None] - levels[:, :, None, :]
    causal = jnp.tril(jnp.ones((BLK, BLK), dtype=bool))[None, None]
    weights = (jnp.where(causal, jnp.exp(jnp.where(causal, spread, 0.0)), 0.0) * scores).astype(
        jnp.bfloat16
    )
    inner_part = jnp.einsum(
        "bhtj,bjhd->bthd", weights, value_blk, preferred_element_type=jnp.float32
    )
    fading = jnp.exp(totals[:, None, :] - cumulative)
    key_faded = (fading[..., None] * key_blk.astype(jnp.float32)).astype(jnp.bfloat16)
    block_states = jnp.einsum(
        "bjhd,bjhe->bhde", key_faded, value_blk, preferred_element_type=jnp.float32
    )

    def advance(running, pair_item):
        total_row, state_row = pair_item
        return (jnp.exp(total_row)[:, None, None] * running + state_row, running)

    empty_state = jnp.zeros((head_count, HEAD_DIM, HEAD_DIM), jnp.float32)
    own_state, local_prev = lax.scan(advance, empty_state, (totals, block_states))
    own_log = jnp.sum(totals, axis=0)
    log_plane = jnp.zeros((1, HEAD_DIM, HEAD_DIM), jnp.bfloat16)
    log_plane = log_plane.at[0, 0, :head_count].set(own_log.astype(jnp.bfloat16))
    payload = jnp.concatenate([own_state.astype(jnp.bfloat16), log_plane], axis=0)
    gathered = lax.all_gather(payload, "seq", axis=0, tiled=False).astype(jnp.float32)
    states_all = gathered[:, :head_count]
    logs_all = gathered[:, head_count, 0, :head_count]
    position = lax.axis_index("seq")
    below_me = jnp.arange(logs_all.shape[0])[:, None] < position
    inclusive = jnp.cumsum(logs_all, axis=0)
    before = jnp.sum(jnp.where(below_me, logs_all, 0.0), axis=0)
    factors = jnp.where(
        below_me, jnp.exp(jnp.where(below_me, before[None, :] - inclusive, 0.0)), 0.0
    )
    incoming = jnp.einsum("sh,shde->hde", factors, states_all, precision=lax.Precision.HIGHEST)
    starts = jnp.concatenate(
        [jnp.zeros((1, head_count), jnp.float32), jnp.cumsum(totals, axis=0)[:-1]], axis=0
    )
    carried = jnp.exp(starts)[:, :, None, None] * incoming[None] + local_prev
    query_faded = jnp.exp(cumulative)[..., None] * query_blk.astype(jnp.float32)
    carried_part = jnp.einsum(
        "bthd,bhde->bthe", query_faded, carried, precision=lax.Precision.HIGHEST
    )
    attention = carried_part + inner_part
    mean_square = jnp.mean(attention * attention, axis=-1, keepdims=True)
    normed = attention * lax.rsqrt(mean_square + 1e-06) * head_gain.reshape(head_count, HEAD_DIM)
    mixed_rows = (residual.astype(jnp.float32) + normed.reshape(token_count, feature_dim)).astype(
        jnp.bfloat16
    )
    token_rows = lax.all_to_all(mixed_rows, "exp", split_axis=0, concat_axis=1, tiled=True)
    row_count, model_dim = token_rows.shape
    token_float = token_rows.astype(jnp.float32)
    row_square = jnp.mean(token_float * token_float, axis=-1, keepdims=True)
    norm_rows = (token_float * lax.rsqrt(row_square + 1e-06) * moe_gain).astype(jnp.bfloat16)
    capacity = row_count * 10 // (4 * EXPERTS)
    flat_ids = routes.reshape(-1)
    onehot = (flat_ids[:, None] == jnp.arange(EXPERTS, dtype=jnp.int32)[None, :]).astype(jnp.int32)
    slot_rank = jnp.sum((jnp.cumsum(onehot, axis=0) - 1) * onehot, axis=1)
    slot_index = flat_ids * capacity + slot_rank
    placer = jnp.arange(EXPERTS * capacity, dtype=jnp.int32)[:, None] == slot_index[None, :]
    placed = placer.reshape(EXPERTS * capacity, row_count, 2)
    packer = jnp.any(placed, axis=2).astype(jnp.bfloat16)
    packed = jnp.dot(packer, norm_rows, preferred_element_type=jnp.float32).astype(jnp.bfloat16)
    combiner = jnp.sum(jnp.where(placed, route_weight[None], 0.0), axis=2)
    exp_count = lax.axis_size("exp")
    local_experts = up_weight.shape[0]
    packed = packed.reshape(exp_count, local_experts, capacity, model_dim)
    summed = []
    for expert in range(local_experts):
        mine = lax.all_to_all(packed[:, expert], "exp", split_axis=0, concat_axis=0, tiled=True)
        mine = mine.reshape(exp_count * capacity, model_dim)
        rows = lax.all_gather(mine, "seq", axis=0, tiled=True)
        partial = expert_part(rows, up_weight[expert], down_weight[expert])
        total = lax.psum_scatter(partial, "seq", scatter_dimension=0, tiled=True)
        total = total.reshape(exp_count, capacity, model_dim)
        summed.append(lax.all_to_all(total, "exp", split_axis=0, concat_axis=0, tiled=True))
    summed = jnp.stack(summed, axis=1).reshape(EXPERTS * capacity, model_dim)
    combined = jnp.dot(
        combiner.T, summed.astype(jnp.float32), precision=lax.Precision.HIGHEST
    )
    return (token_float + combined).astype(jnp.bfloat16)


def solution(mesh):
    return jax.shard_map(
        per_device,
        mesh=mesh,
        in_specs=(
            P("seq", "exp"),
            P("seq", "exp"),
            P("seq", "exp"),
            P("seq", "exp"),
            P("seq", "exp"),
            P("exp"),
            P(),
            P(("seq", "exp"), None),
            P(("seq", "exp"), None),
            P("exp", None, "seq"),
            P("exp", "seq", None),
        ),
        out_specs=P(("seq", "exp"), None),
        check_vma=False,
    )
```

```python
import jax
import jax.numpy as jnp
from jax import lax
from jax.experimental import pallas as pl
from jax.experimental.pallas import tpu as pltpu
from jax.sharding import PartitionSpec as P

HEAD_DIM = 128
BLK = 256
EXPERTS = 8


MESH = pl.DeviceIdType.MESH
Z_LEN = 4


def chip_place():
    seq, exp = lax.axis_index("seq"), lax.axis_index("exp")
    z, y, x, c = lax.div(seq, 2), lax.rem(seq, 2), lax.div(exp, 2), lax.rem(exp, 2)

    def block(shift, jy, jx, jc):
        zz = lax.rem(z + shift + Z_LEN, Z_LEN)
        yy, xx, cc = lax.rem(y + jy, 2), lax.rem(x + jx, 2), lax.rem(c + jc, 2)
        return (zz * 2 + yy) * 4 + xx * 2 + cc

    def device(shift, jy, jx, jc):
        index = block(shift, jy, jx, jc)
        return (lax.div(index, 4), lax.rem(index, 4))

    return block, device


def greet(device):
    barrier = pltpu.get_barrier_semaphore()
    peers = [device(1, 0, 0, 0), device(2, 0, 0, 0), device(3, 0, 0, 0)]
    peers += [device(0, 1, 0, 0), device(0, 0, 1, 0), device(0, 0, 0, 1)]
    for peer in peers:
        pl.semaphore_signal(barrier, inc=1, device_id=peer, device_id_type=MESH)
    pl.semaphore_wait(barrier, len(peers))


def gather_kernel(own_ref, out_ref, send_sem, recv_sem, local_sem):
    block, device = chip_place()
    half = own_ref.shape[1] // 2
    left, right = pl.ds(0, half), pl.ds(half, half)
    greet(device)
    copies = {}

    def send(name, src, dst, peer):
        spot = len(copies)
        copies[name] = pltpu.make_async_remote_copy(
            src_ref=src,
            dst_ref=dst,
            send_sem=send_sem.at[spot],
            recv_sem=recv_sem.at[spot],
            device_id=peer,
            device_id_type=MESH,
        )
        copies[name].start()

    y_peer, x_peer, twin = device(0, 1, 0, 0), device(0, 0, 1, 0), device(0, 0, 0, 1)
    mine = out_ref.at[block(0, 0, 0, 0)]
    keep = pltpu.make_async_copy(own_ref, mine, local_sem)
    keep.start()

    def spread_diagonal(k):
        there = out_ref.at[block(-k, 1, 1, 0)]
        copies["da", k].wait_recv()
        send(("ta", k), there.at[:, left], there.at[:, left], twin)
        copies["db", k].wait_recv()
        send(("tb", k), there.at[:, right], there.at[:, right], twin)

    order = (0, 1, 3, 2)
    for turn, k in enumerate(order):
        spot = out_ref.at[block(-k, 0, 0, 0)]
        if k:
            copies["z", k].wait_recv()
        src = spot if k else own_ref
        send(("y", k), src, spot, y_peer)
        send(("x", k), src, spot, x_peer)
        if turn + 1 < len(order):
            later = order[turn + 1]
            send(("z", later), own_ref, mine, device(later, 0, 0, 0))
        send(("t", k), src, spot, twin)
        if turn:
            spread_diagonal(order[turn - 1])
        from_y = out_ref.at[block(-k, 1, 0, 0)]
        from_x = out_ref.at[block(-k, 0, 1, 0)]
        copies["y", k].wait_recv()
        send(("da", k), from_y.at[:, left], from_y.at[:, left], x_peer)
        copies["x", k].wait_recv()
        send(("db", k), from_x.at[:, right], from_x.at[:, right], y_peer)
        send(("ty", k), from_y, from_y, twin)
        send(("tx", k), from_x, from_x, twin)
    spread_diagonal(order[-1])
    for name, copy in copies.items():
        copy.wait_send()
        if name[0] in ("t", "ty", "tx", "ta", "tb"):
            copy.wait_recv()
    keep.wait()


def gather_rows(rows, block_total):
    row_count, width = rows.shape
    return pl.pallas_call(
        gather_kernel,
        out_shape=jax.ShapeDtypeStruct((block_total, row_count, width), rows.dtype),
        in_specs=[pl.BlockSpec(memory_space=pl.ANY)],
        out_specs=pl.BlockSpec(memory_space=pl.ANY),
        scratch_shapes=[
            pltpu.SemaphoreType.DMA((39,)),
            pltpu.SemaphoreType.DMA((39,)),
            pltpu.SemaphoreType.DMA,
        ],
        compiler_params=pltpu.CompilerParams(collective_id=0, has_side_effects=True),
        name="gather_rows",
    )(rows)


def reduce_kernel(part_ref, out_ref, mine, twin_in, diag_in, y_in, x_in, z_in, send_sem, recv_sem, load_sem):
    block, device = chip_place()
    row_count, width = out_ref.shape
    half = width // 2
    full, left, right = pl.ds(0, width), pl.ds(0, half), pl.ds(half, half)
    tile = 16
    greet(device)
    copies = {}

    def send(name, src, dst, peer):
        spot = len(copies)
        copies[name] = pltpu.make_async_remote_copy(
            src_ref=src,
            dst_ref=dst,
            send_sem=send_sem.at[spot],
            recv_sem=recv_sem.at[spot],
            device_id=peer,
            device_id_type=MESH,
        )
        copies[name].start()

    def add_into(target, sources, columns):
        @pl.loop(0, row_count // tile)
        def _(step):
            rows = pl.ds(step * tile, tile)
            total = target[rows, columns].astype(jnp.float32)
            for source in sources:
                total = total + source[rows, columns].astype(jnp.float32)
            target[rows, columns] = total.astype(target.dtype)

    y_peer, x_peer, twin = device(0, 1, 0, 0), device(0, 0, 1, 0), device(0, 0, 0, 1)
    order = (2, 1, 3, 0)
    loads = {}
    for turn, k in enumerate(order):
        for q in (3, 2, 1, 0):
            spot = turn * 4 + q
            theirs = part_ref.at[block(k, q // 2, q % 2, 1)]
            send(("t", spot), theirs, twin_in.at[spot], twin)
            loads[spot] = pltpu.make_async_copy(
                part_ref.at[block(k, q // 2, q % 2, 0)], mine.at[spot], load_sem.at[spot]
            )
            loads[spot].start()

    def join_twin(turn):
        for q in (3, 2, 1, 0):
            spot = turn * 4 + q
            loads[spot].wait()
            copies["t", spot].wait_recv()
            add_into(mine.at[spot], [twin_in.at[spot]], full)
            if q == 3:
                source, target = mine.at[spot], diag_in.at[turn]
                send(("da", turn), source.at[:, left], target.at[:, left], x_peer)
                send(("db", turn), source.at[:, right], target.at[:, right], y_peer)

    def join_diagonal(turn):
        copies["da", turn].wait_recv()
        add_into(mine.at[turn * 4 + 2], [diag_in.at[turn]], left)
        send(("y", turn), mine.at[turn * 4 + 2], y_in.at[turn], y_peer)
        copies["db", turn].wait_recv()
        add_into(mine.at[turn * 4 + 1], [diag_in.at[turn]], right)
        send(("x", turn), mine.at[turn * 4 + 1], x_in.at[turn], x_peer)

    def join_sides(turn):
        copies["y", turn].wait_recv()
        copies["x", turn].wait_recv()
        add_into(mine.at[turn * 4], [y_in.at[turn], x_in.at[turn]], full)
        if order[turn]:
            send(("z", turn), mine.at[turn * 4], z_in.at[turn], device(order[turn], 0, 0, 0))

    for turn in range(len(order) + 2):
        if turn < len(order):
            join_twin(turn)
        if 0 <= turn - 1 < len(order):
            join_diagonal(turn - 1)
        if 0 <= turn - 2:
            join_sides(turn - 2)
    for turn in range(3):
        copies["z", turn].wait_recv()
    last = mine.at[12]

    @pl.loop(0, row_count // tile)
    def _(step):
        rows = pl.ds(step * tile, tile)
        total = last[rows, :].astype(jnp.float32)
        for turn in range(3):
            total = total + z_in[turn, rows, :].astype(jnp.float32)
        out_ref[rows, :] = total

    for copy in copies.values():
        copy.wait_send()


def reduce_rows(parts):
    block_total, row_count, width = parts.shape
    many = lambda n: pltpu.VMEM((n, row_count, width), parts.dtype)
    return pl.pallas_call(
        reduce_kernel,
        out_shape=jax.ShapeDtypeStruct((row_count, width), jnp.float32),
        in_specs=[pl.BlockSpec(memory_space=pl.ANY)],
        out_specs=pl.BlockSpec(memory_space=pltpu.VMEM),
        scratch_shapes=[
            many(16),
            many(16),
            many(4),
            many(4),
            many(4),
            many(3),
            pltpu.SemaphoreType.DMA((35,)),
            pltpu.SemaphoreType.DMA((35,)),
            pltpu.SemaphoreType.DMA((16,)),
        ],
        compiler_params=pltpu.CompilerParams(
            collective_id=1, has_side_effects=True, vmem_limit_bytes=56 * 1024 * 1024
        ),
        name="reduce_rows",
    )(parts)


def experts_by_kernels(norm_rows, routes, route_weight, up_weight, down_weight, capacity):
    row_count, model_dim = norm_rows.shape
    seq_count, exp_count = lax.axis_size("seq"), lax.axis_size("exp")
    block_total = seq_count * exp_count
    local_experts = up_weight.shape[0]
    sheet = jnp.concatenate([routes.astype(jnp.float32), route_weight], axis=1).T
    sheets = lax.all_gather(sheet, ("seq", "exp"), axis=0, tiled=False)
    first = lax.axis_index("exp") * local_experts
    local_ids = (first + jnp.arange(local_experts)).astype(jnp.float32)[:, None, None, None]
    hits = sheets[None, :, :2] == local_ids
    member = jnp.any(hits, axis=2)
    member_weight = jnp.sum(jnp.where(hits, sheets[None, :, 2:], 0.0), axis=2)
    earlier = jnp.triu(jnp.ones((row_count, row_count), jnp.bfloat16), 1)
    rank = jnp.einsum(
        "lbt,tu->lbu",
        member.astype(jnp.bfloat16),
        earlier,
        preferred_element_type=jnp.float32,
    ).astype(jnp.int32)
    slot = rank + (jnp.arange(block_total, dtype=jnp.int32) % exp_count)[None, :, None] * capacity
    grouped = (local_experts, seq_count, 1, exp_count * row_count)
    slots = exp_count * capacity
    pick = (jnp.arange(slots, dtype=jnp.int32)[:, None] == slot.reshape(grouped)) & member.reshape(
        grouped
    )
    slot_weight = jnp.sum(jnp.where(pick, member_weight.reshape(grouped), 0.0), axis=3)
    pick = pick.astype(jnp.bfloat16)
    rows = gather_rows(norm_rows, block_total)
    rows = rows.reshape(seq_count, exp_count * row_count, model_dim)
    parts = []
    for expert in range(local_experts):
        packed = jnp.einsum(
            "gst,gtd->gsd", pick[expert], rows, preferred_element_type=jnp.float32
        ).astype(jnp.bfloat16)
        packed = packed.reshape(seq_count * slots, model_dim)
        hidden = jax.nn.silu(
            jnp.dot(packed, up_weight[expert], preferred_element_type=jnp.float32)
        ).astype(jnp.bfloat16)
        part = jnp.dot(hidden, down_weight[expert], preferred_element_type=jnp.float32)
        part = (part * slot_weight[expert].reshape(-1, 1)).astype(jnp.bfloat16)
        parts.append(part.reshape(seq_count, slots, model_dim))
    spread = sum(
        jnp.einsum("gst,gsd->gtd", pick[expert], parts[expert], preferred_element_type=jnp.float32)
        for expert in range(local_experts)
    ).astype(jnp.bfloat16)
    return reduce_rows(spread.reshape(block_total, row_count, model_dim))


def expert_part(rows, up_weight, down_weight):
    hidden = jax.nn.silu(jnp.dot(rows, up_weight, preferred_element_type=jnp.float32)).astype(
        jnp.bfloat16
    )
    return jnp.dot(hidden, down_weight, preferred_element_type=jnp.float32).astype(jnp.bfloat16)


def per_device(
    queries,
    key_rows,
    value_rows,
    log_decay,
    residual,
    head_gain,
    moe_gain,
    routes,
    route_weight,
    up_weight,
    down_weight,
):
    token_count, feature_dim = queries.shape
    head_count = log_decay.shape[1]
    block_count = token_count // BLK
    shaped = (block_count, BLK, head_count, HEAD_DIM)
    query_blk = queries.reshape(shaped)
    key_blk = key_rows.reshape(shaped)
    value_blk = value_rows.reshape(shaped)
    cumulative = jnp.cumsum(log_decay.reshape(block_count, BLK, head_count), axis=1)
    totals = cumulative[:, -1, :]
    scores = jnp.einsum("bthd,bjhd->bhtj", query_blk, key_blk, preferred_element_type=jnp.float32)
    levels = jnp.transpose(cumulative, (0, 2, 1))
    spread = levels[:, :, :, None] - levels[:, :, None, :]
    causal = jnp.tril(jnp.ones((BLK, BLK), dtype=bool))[None, None]
    weights = (jnp.where(causal, jnp.exp(jnp.where(causal, spread, 0.0)), 0.0) * scores).astype(
        jnp.bfloat16
    )
    inner_part = jnp.einsum(
        "bhtj,bjhd->bthd", weights, value_blk, preferred_element_type=jnp.float32
    )
    fading = jnp.exp(totals[:, None, :] - cumulative)
    key_faded = (fading[..., None] * key_blk.astype(jnp.float32)).astype(jnp.bfloat16)
    block_states = jnp.einsum(
        "bjhd,bjhe->bhde", key_faded, value_blk, preferred_element_type=jnp.float32
    )

    def advance(running, pair_item):
        total_row, state_row = pair_item
        return (jnp.exp(total_row)[:, None, None] * running + state_row, running)

    empty_state = jnp.zeros((head_count, HEAD_DIM, HEAD_DIM), jnp.float32)
    own_state, local_prev = lax.scan(advance, empty_state, (totals, block_states))
    own_log = jnp.sum(totals, axis=0)
    log_plane = jnp.zeros((1, HEAD_DIM, HEAD_DIM), jnp.bfloat16)
    log_plane = log_plane.at[0, 0, :head_count].set(own_log.astype(jnp.bfloat16))
    payload = jnp.concatenate([own_state.astype(jnp.bfloat16), log_plane], axis=0)
    gathered = lax.all_gather(payload, "seq", axis=0, tiled=False).astype(jnp.float32)
    states_all = gathered[:, :head_count]
    logs_all = gathered[:, head_count, 0, :head_count]
    position = lax.axis_index("seq")
    below_me = jnp.arange(logs_all.shape[0])[:, None] < position
    inclusive = jnp.cumsum(logs_all, axis=0)
    before = jnp.sum(jnp.where(below_me, logs_all, 0.0), axis=0)
    factors = jnp.where(
        below_me, jnp.exp(jnp.where(below_me, before[None, :] - inclusive, 0.0)), 0.0
    )
    incoming = jnp.einsum("sh,shde->hde", factors, states_all, precision=lax.Precision.HIGHEST)
    starts = jnp.concatenate(
        [jnp.zeros((1, head_count), jnp.float32), jnp.cumsum(totals, axis=0)[:-1]], axis=0
    )
    carried = jnp.exp(starts)[:, :, None, None] * incoming[None] + local_prev
    query_faded = jnp.exp(cumulative)[..., None] * query_blk.astype(jnp.float32)
    carried_part = jnp.einsum(
        "bthd,bhde->bthe", query_faded, carried, precision=lax.Precision.HIGHEST
    )
    attention = carried_part + inner_part
    mean_square = jnp.mean(attention * attention, axis=-1, keepdims=True)
    normed = attention * lax.rsqrt(mean_square + 1e-06) * head_gain.reshape(head_count, HEAD_DIM)
    mixed_rows = (residual.astype(jnp.float32) + normed.reshape(token_count, feature_dim)).astype(
        jnp.bfloat16
    )
    token_rows = lax.all_to_all(mixed_rows, "exp", split_axis=0, concat_axis=1, tiled=True)
    row_count, model_dim = token_rows.shape
    token_float = token_rows.astype(jnp.float32)
    row_square = jnp.mean(token_float * token_float, axis=-1, keepdims=True)
    norm_rows = (token_float * lax.rsqrt(row_square + 1e-06) * moe_gain).astype(jnp.bfloat16)
    capacity = row_count * 10 // (4 * EXPERTS)
    if (lax.axis_size("seq"), lax.axis_size("exp")) == (2 * Z_LEN, 4):
        combined = experts_by_kernels(
            norm_rows, routes, route_weight, up_weight, down_weight, capacity
        )
        return (token_float + combined).astype(jnp.bfloat16)
    flat_ids = routes.reshape(-1)
    onehot = (flat_ids[:, None] == jnp.arange(EXPERTS, dtype=jnp.int32)[None, :]).astype(jnp.int32)
    slot_rank = jnp.sum((jnp.cumsum(onehot, axis=0) - 1) * onehot, axis=1)
    slot_index = flat_ids * capacity + slot_rank
    placer = jnp.arange(EXPERTS * capacity, dtype=jnp.int32)[:, None] == slot_index[None, :]
    placed = placer.reshape(EXPERTS * capacity, row_count, 2)
    packer = jnp.any(placed, axis=2).astype(jnp.bfloat16)
    packed = jnp.dot(packer, norm_rows, preferred_element_type=jnp.float32).astype(jnp.bfloat16)
    combiner = jnp.sum(jnp.where(placed, route_weight[None], 0.0), axis=2)
    exp_count = lax.axis_size("exp")
    local_experts = up_weight.shape[0]
    packed = packed.reshape(exp_count, local_experts, capacity, model_dim)
    summed = []
    for expert in range(local_experts):
        mine = lax.all_to_all(packed[:, expert], "exp", split_axis=0, concat_axis=0, tiled=True)
        mine = mine.reshape(exp_count * capacity, model_dim)
        rows = lax.all_gather(mine, "seq", axis=0, tiled=True)
        partial = expert_part(rows, up_weight[expert], down_weight[expert])
        total = lax.psum_scatter(partial, "seq", scatter_dimension=0, tiled=True)
        total = total.reshape(exp_count, capacity, model_dim)
        summed.append(lax.all_to_all(total, "exp", split_axis=0, concat_axis=0, tiled=True))
    summed = jnp.stack(summed, axis=1).reshape(EXPERTS * capacity, model_dim)
    combined = jnp.dot(
        combiner.T, summed.astype(jnp.float32), precision=lax.Precision.HIGHEST
    )
    return (token_float + combined).astype(jnp.bfloat16)


def solution(mesh):
    return jax.shard_map(
        per_device,
        mesh=mesh,
        in_specs=(
            P("seq", "exp"),
            P("seq", "exp"),
            P("seq", "exp"),
            P("seq", "exp"),
            P("seq", "exp"),
            P("exp"),
            P(),
            P(("seq", "exp"), None),
            P(("seq", "exp"), None),
            P("exp", None, "seq"),
            P("exp", "seq", None),
        ),
        out_specs=P(("seq", "exp"), None),
        check_vma=False,
    )
```

```python
import jax
import jax.numpy as jnp
from jax import lax
from jax.experimental import pallas as pl
from jax.experimental.pallas import tpu as pltpu
from jax.sharding import PartitionSpec as P

HEAD_DIM = 128
BLK = 256
EXPERTS = 8


MESH = pl.DeviceIdType.MESH
Z_LEN = 4


def chip_place():
    seq, exp = lax.axis_index("seq"), lax.axis_index("exp")
    z, y, x, c = lax.div(seq, 2), lax.rem(seq, 2), lax.div(exp, 2), lax.rem(exp, 2)

    def block(shift, jy, jx, jc):
        zz = lax.rem(z + shift + Z_LEN, Z_LEN)
        yy, xx, cc = lax.rem(y + jy, 2), lax.rem(x + jx, 2), lax.rem(c + jc, 2)
        return (zz * 2 + yy) * 4 + xx * 2 + cc

    def device(shift, jy, jx, jc):
        index = block(shift, jy, jx, jc)
        return (lax.div(index, 4), lax.rem(index, 4))

    return block, device


def greet(device):
    barrier = pltpu.get_barrier_semaphore()
    peers = [device(1, 0, 0, 0), device(2, 0, 0, 0), device(3, 0, 0, 0)]
    peers += [device(0, 1, 0, 0), device(0, 0, 1, 0), device(0, 0, 0, 1)]
    for peer in peers:
        pl.semaphore_signal(barrier, inc=1, device_id=peer, device_id_type=MESH)
    pl.semaphore_wait(barrier, len(peers))


def gather_up_kernel(
    own_ref,
    share_ref,
    weight_ref,
    out_ref,
    hidden_ref,
    weights,
    rows_in,
    total,
    send_sem,
    recv_sem,
    local_sem,
    load_sem,
    weight_sem,
):
    block, device = chip_place()
    half = own_ref.shape[1] // 2
    left, right = pl.ds(0, half), pl.ds(half, half)
    greet(device)
    copies = {}

    def send(name, src, dst, peer):
        spot = len(copies)
        copies[name] = pltpu.make_async_remote_copy(
            src_ref=src,
            dst_ref=dst,
            send_sem=send_sem.at[spot],
            recv_sem=recv_sem.at[spot],
            device_id=peer,
            device_id_type=MESH,
        )
        copies[name].start()

    y_peer, x_peer, twin = device(0, 1, 0, 0), device(0, 0, 1, 0), device(0, 0, 0, 1)
    mine = out_ref.at[block(0, 0, 0, 0)]
    keep = pltpu.make_async_copy(own_ref, mine, local_sem)
    keep.start()

    expert_count, depth, hidden_width = weight_ref.shape
    weight_copy = pltpu.make_async_copy(weight_ref, weights, weight_sem)
    row_count = own_ref.shape[0]
    step_depth = 512

    def compute(k, jy):
        names = [("ty", k), ("ta", k), ("tb", k)] if jy else [("t", k), ("tx", k)]
        for name in names:
            copies[name].wait_recv()
        if (k, jy) == (0, 0):
            weight_copy.wait()
            keep.wait()
        spots = [block(-k, jy, jx, jc) for jx in range(2) for jc in range(2)]
        loads = []
        for place, spot in enumerate(spots):
            load = pltpu.make_async_copy(
                out_ref.at[spot],
                rows_in.at[pl.ds(place * row_count, row_count)],
                load_sem.at[place],
            )
            load.start()
            loads.append(load)
        for load in loads:
            load.wait()
        for expert in range(expert_count):
            total[...] = jnp.zeros_like(total)

            @pl.loop(0, depth // step_depth)
            def _(step):
                span = pl.ds(pl.multiple_of(step * step_depth, step_depth), step_depth)
                total[...] += jnp.dot(
                    rows_in[:, span],
                    weights[expert, span, :],
                    preferred_element_type=jnp.float32,
                )

            for place, spot in enumerate(spots):
                up = total[place * row_count : (place + 1) * row_count, :]
                share = share_ref[spot][:, expert : expert + 1]
                hidden = up / (1.0 + jnp.exp(-up)) * share
                hidden_ref[spot, :, pl.ds(expert * hidden_width, hidden_width)] = hidden.astype(
                    hidden_ref.dtype
                )

    def spread_diagonal(k):
        there = out_ref.at[block(-k, 1, 1, 0)]
        copies["da", k].wait_recv()
        send(("ta", k), there.at[:, left], there.at[:, left], twin)
        copies["db", k].wait_recv()
        send(("tb", k), there.at[:, right], there.at[:, right], twin)

    order = (0, 1, 3, 2)
    for turn, k in enumerate(order):
        spot = out_ref.at[block(-k, 0, 0, 0)]
        if k:
            copies["z", k].wait_recv()
        src = spot if k else own_ref
        send(("y", k), src, spot, y_peer)
        send(("x", k), src, spot, x_peer)
        if turn + 1 < len(order):
            later = order[turn + 1]
            send(("z", later), own_ref, mine, device(later, 0, 0, 0))
        send(("t", k), src, spot, twin)
        if turn:
            spread_diagonal(order[turn - 1])
            compute(order[turn - 1], 0)
        else:
            weight_copy.start()
        from_y = out_ref.at[block(-k, 1, 0, 0)]
        from_x = out_ref.at[block(-k, 0, 1, 0)]
        copies["y", k].wait_recv()
        send(("da", k), from_y.at[:, left], from_y.at[:, left], x_peer)
        copies["x", k].wait_recv()
        send(("db", k), from_x.at[:, right], from_x.at[:, right], y_peer)
        send(("ty", k), from_y, from_y, twin)
        send(("tx", k), from_x, from_x, twin)
        if turn:
            compute(order[turn - 1], 1)
    compute(order[-1], 0)
    spread_diagonal(order[-1])
    compute(order[-1], 1)
    for copy in copies.values():
        copy.wait_send()


def gather_up(rows, shares, up_weight):
    block_total = shares.shape[0]
    row_count, width = rows.shape
    expert_count, _, hidden_width = up_weight.shape
    _, hidden = pl.pallas_call(
        gather_up_kernel,
        out_shape=[
            jax.ShapeDtypeStruct((block_total, row_count, width), rows.dtype),
            jax.ShapeDtypeStruct((block_total, row_count, expert_count * hidden_width), rows.dtype),
        ],
        in_specs=[
            pl.BlockSpec(memory_space=pl.ANY),
            pl.BlockSpec(memory_space=pltpu.VMEM),
            pl.BlockSpec(memory_space=pl.ANY),
        ],
        out_specs=[pl.BlockSpec(memory_space=pl.ANY), pl.BlockSpec(memory_space=pltpu.VMEM)],
        scratch_shapes=[
            pltpu.VMEM(up_weight.shape, up_weight.dtype),
            pltpu.VMEM((4 * row_count, width), rows.dtype),
            pltpu.VMEM((4 * row_count, hidden_width), jnp.float32),
            pltpu.SemaphoreType.DMA((39,)),
            pltpu.SemaphoreType.DMA((39,)),
            pltpu.SemaphoreType.DMA,
            pltpu.SemaphoreType.DMA((4,)),
            pltpu.SemaphoreType.DMA,
        ],
        compiler_params=pltpu.CompilerParams(
            collective_id=0, has_side_effects=True, vmem_limit_bytes=56 * 1024 * 1024
        ),
        name="gather_up",
    )(rows, shares, up_weight)
    return hidden


def reduce_kernel(part_ref, out_ref, mine, twin_in, diag_in, y_in, x_in, z_in, send_sem, recv_sem, load_sem):
    block, device = chip_place()
    row_count, width = out_ref.shape
    half = width // 2
    full, left, right = pl.ds(0, width), pl.ds(0, half), pl.ds(half, half)
    tile = 16
    greet(device)
    copies = {}

    def send(name, src, dst, peer):
        spot = len(copies)
        copies[name] = pltpu.make_async_remote_copy(
            src_ref=src,
            dst_ref=dst,
            send_sem=send_sem.at[spot],
            recv_sem=recv_sem.at[spot],
            device_id=peer,
            device_id_type=MESH,
        )
        copies[name].start()

    def add_into(target, sources, columns):
        @pl.loop(0, row_count // tile)
        def _(step):
            rows = pl.ds(step * tile, tile)
            total = target[rows, columns].astype(jnp.float32)
            for source in sources:
                total = total + source[rows, columns].astype(jnp.float32)
            target[rows, columns] = total.astype(target.dtype)

    y_peer, x_peer, twin = device(0, 1, 0, 0), device(0, 0, 1, 0), device(0, 0, 0, 1)
    order = (2, 1, 3, 0)
    loads = {}
    for turn, k in enumerate(order):
        for q in (3, 2, 1, 0):
            spot = turn * 4 + q
            theirs = part_ref.at[block(k, q // 2, q % 2, 1)]
            send(("t", spot), theirs, twin_in.at[spot], twin)
            loads[spot] = pltpu.make_async_copy(
                part_ref.at[block(k, q // 2, q % 2, 0)], mine.at[spot], load_sem.at[spot]
            )
            loads[spot].start()

    def join_twin(turn):
        for q in (3, 2, 1, 0):
            spot = turn * 4 + q
            loads[spot].wait()
            copies["t", spot].wait_recv()
            add_into(mine.at[spot], [twin_in.at[spot]], full)
            if q == 3:
                source, target = mine.at[spot], diag_in.at[turn]
                send(("da", turn), source.at[:, left], target.at[:, left], x_peer)
                send(("db", turn), source.at[:, right], target.at[:, right], y_peer)

    def join_diagonal(turn):
        copies["da", turn].wait_recv()
        add_into(mine.at[turn * 4 + 2], [diag_in.at[turn]], left)
        send(("y", turn), mine.at[turn * 4 + 2], y_in.at[turn], y_peer)
        copies["db", turn].wait_recv()
        add_into(mine.at[turn * 4 + 1], [diag_in.at[turn]], right)
        send(("x", turn), mine.at[turn * 4 + 1], x_in.at[turn], x_peer)

    def join_sides(turn):
        copies["y", turn].wait_recv()
        copies["x", turn].wait_recv()
        add_into(mine.at[turn * 4], [y_in.at[turn], x_in.at[turn]], full)
        if order[turn]:
            send(("z", turn), mine.at[turn * 4], z_in.at[turn], device(order[turn], 0, 0, 0))

    for turn in range(len(order) + 2):
        if turn < len(order):
            join_twin(turn)
        if 0 <= turn - 1 < len(order):
            join_diagonal(turn - 1)
        if 0 <= turn - 2:
            join_sides(turn - 2)
    for turn in range(3):
        copies["z", turn].wait_recv()
    last = mine.at[12]

    @pl.loop(0, row_count // tile)
    def _(step):
        rows = pl.ds(step * tile, tile)
        total = last[rows, :].astype(jnp.float32)
        for turn in range(3):
            total = total + z_in[turn, rows, :].astype(jnp.float32)
        out_ref[rows, :] = total

    for copy in copies.values():
        copy.wait_send()


def reduce_rows(parts):
    block_total, row_count, width = parts.shape
    many = lambda n: pltpu.VMEM((n, row_count, width), parts.dtype)
    return pl.pallas_call(
        reduce_kernel,
        out_shape=jax.ShapeDtypeStruct((row_count, width), jnp.float32),
        in_specs=[pl.BlockSpec(memory_space=pl.ANY)],
        out_specs=pl.BlockSpec(memory_space=pltpu.VMEM),
        scratch_shapes=[
            many(16),
            many(16),
            many(4),
            many(4),
            many(4),
            many(3),
            pltpu.SemaphoreType.DMA((35,)),
            pltpu.SemaphoreType.DMA((35,)),
            pltpu.SemaphoreType.DMA((16,)),
        ],
        compiler_params=pltpu.CompilerParams(
            collective_id=1, has_side_effects=True, vmem_limit_bytes=56 * 1024 * 1024
        ),
        name="reduce_rows",
    )(parts)


def experts_by_kernels(norm_rows, routes, route_weight, up_weight, down_weight):
    row_count, model_dim = norm_rows.shape
    local_experts, hidden_width, _ = down_weight.shape
    sheet = jnp.concatenate([routes.astype(jnp.float32), route_weight], axis=1).T
    sheets = lax.all_gather(sheet, ("seq", "exp"), axis=0, tiled=False)
    first = lax.axis_index("exp") * local_experts
    local_ids = (first + jnp.arange(local_experts)).astype(jnp.float32)
    hits = sheets[:, :2, :, None] == local_ids
    shares = jnp.sum(jnp.where(hits, sheets[:, 2:, :, None], 0.0), axis=1)
    hidden = gather_up(norm_rows, shares, up_weight)
    spread = jnp.dot(
        hidden.reshape(-1, local_experts * hidden_width),
        down_weight.reshape(local_experts * hidden_width, model_dim),
        preferred_element_type=jnp.float32,
    ).astype(jnp.bfloat16)
    return reduce_rows(spread.reshape(-1, row_count, model_dim))


def expert_part(rows, up_weight, down_weight):
    hidden = jax.nn.silu(jnp.dot(rows, up_weight, preferred_element_type=jnp.float32)).astype(
        jnp.bfloat16
    )
    return jnp.dot(hidden, down_weight, preferred_element_type=jnp.float32).astype(jnp.bfloat16)


def per_device(
    queries,
    key_rows,
    value_rows,
    log_decay,
    residual,
    head_gain,
    moe_gain,
    routes,
    route_weight,
    up_weight,
    down_weight,
):
    token_count, feature_dim = queries.shape
    head_count = log_decay.shape[1]
    block_count = token_count // BLK
    shaped = (block_count, BLK, head_count, HEAD_DIM)
    query_blk = queries.reshape(shaped)
    key_blk = key_rows.reshape(shaped)
    value_blk = value_rows.reshape(shaped)
    cumulative = jnp.cumsum(log_decay.reshape(block_count, BLK, head_count), axis=1)
    totals = cumulative[:, -1, :]
    scores = jnp.einsum("bthd,bjhd->bhtj", query_blk, key_blk, preferred_element_type=jnp.float32)
    levels = jnp.transpose(cumulative, (0, 2, 1))
    spread = levels[:, :, :, None] - levels[:, :, None, :]
    causal = jnp.tril(jnp.ones((BLK, BLK), dtype=bool))[None, None]
    weights = (jnp.where(causal, jnp.exp(jnp.where(causal, spread, 0.0)), 0.0) * scores).astype(
        jnp.bfloat16
    )
    inner_part = jnp.einsum(
        "bhtj,bjhd->bthd", weights, value_blk, preferred_element_type=jnp.float32
    )
    fading = jnp.exp(totals[:, None, :] - cumulative)
    key_faded = (fading[..., None] * key_blk.astype(jnp.float32)).astype(jnp.bfloat16)
    block_states = jnp.einsum(
        "bjhd,bjhe->bhde", key_faded, value_blk, preferred_element_type=jnp.float32
    )

    def advance(running, pair_item):
        total_row, state_row = pair_item
        return (jnp.exp(total_row)[:, None, None] * running + state_row, running)

    empty_state = jnp.zeros((head_count, HEAD_DIM, HEAD_DIM), jnp.float32)
    own_state, local_prev = lax.scan(advance, empty_state, (totals, block_states))
    own_log = jnp.sum(totals, axis=0)
    log_plane = jnp.zeros((1, HEAD_DIM, HEAD_DIM), jnp.bfloat16)
    log_plane = log_plane.at[0, 0, :head_count].set(own_log.astype(jnp.bfloat16))
    payload = jnp.concatenate([own_state.astype(jnp.bfloat16), log_plane], axis=0)
    gathered = lax.all_gather(payload, "seq", axis=0, tiled=False).astype(jnp.float32)
    states_all = gathered[:, :head_count]
    logs_all = gathered[:, head_count, 0, :head_count]
    position = lax.axis_index("seq")
    below_me = jnp.arange(logs_all.shape[0])[:, None] < position
    inclusive = jnp.cumsum(logs_all, axis=0)
    before = jnp.sum(jnp.where(below_me, logs_all, 0.0), axis=0)
    factors = jnp.where(
        below_me, jnp.exp(jnp.where(below_me, before[None, :] - inclusive, 0.0)), 0.0
    )
    incoming = jnp.einsum("sh,shde->hde", factors, states_all, precision=lax.Precision.HIGHEST)
    starts = jnp.concatenate(
        [jnp.zeros((1, head_count), jnp.float32), jnp.cumsum(totals, axis=0)[:-1]], axis=0
    )
    carried = jnp.exp(starts)[:, :, None, None] * incoming[None] + local_prev
    query_faded = jnp.exp(cumulative)[..., None] * query_blk.astype(jnp.float32)
    carried_part = jnp.einsum(
        "bthd,bhde->bthe", query_faded, carried, precision=lax.Precision.HIGHEST
    )
    attention = carried_part + inner_part
    mean_square = jnp.mean(attention * attention, axis=-1, keepdims=True)
    normed = attention * lax.rsqrt(mean_square + 1e-06) * head_gain.reshape(head_count, HEAD_DIM)
    mixed_rows = (residual.astype(jnp.float32) + normed.reshape(token_count, feature_dim)).astype(
        jnp.bfloat16
    )
    token_rows = lax.all_to_all(mixed_rows, "exp", split_axis=0, concat_axis=1, tiled=True)
    row_count, model_dim = token_rows.shape
    token_float = token_rows.astype(jnp.float32)
    row_square = jnp.mean(token_float * token_float, axis=-1, keepdims=True)
    norm_rows = (token_float * lax.rsqrt(row_square + 1e-06) * moe_gain).astype(jnp.bfloat16)
    capacity = row_count * 10 // (4 * EXPERTS)
    if (lax.axis_size("seq"), lax.axis_size("exp")) == (2 * Z_LEN, 4):
        combined = experts_by_kernels(norm_rows, routes, route_weight, up_weight, down_weight)
        return (token_float + combined).astype(jnp.bfloat16)
    flat_ids = routes.reshape(-1)
    onehot = (flat_ids[:, None] == jnp.arange(EXPERTS, dtype=jnp.int32)[None, :]).astype(jnp.int32)
    slot_rank = jnp.sum((jnp.cumsum(onehot, axis=0) - 1) * onehot, axis=1)
    slot_index = flat_ids * capacity + slot_rank
    placer = jnp.arange(EXPERTS * capacity, dtype=jnp.int32)[:, None] == slot_index[None, :]
    placed = placer.reshape(EXPERTS * capacity, row_count, 2)
    packer = jnp.any(placed, axis=2).astype(jnp.bfloat16)
    packed = jnp.dot(packer, norm_rows, preferred_element_type=jnp.float32).astype(jnp.bfloat16)
    combiner = jnp.sum(jnp.where(placed, route_weight[None], 0.0), axis=2)
    exp_count = lax.axis_size("exp")
    local_experts = up_weight.shape[0]
    packed = packed.reshape(exp_count, local_experts, capacity, model_dim)
    summed = []
    for expert in range(local_experts):
        mine = lax.all_to_all(packed[:, expert], "exp", split_axis=0, concat_axis=0, tiled=True)
        mine = mine.reshape(exp_count * capacity, model_dim)
        rows = lax.all_gather(mine, "seq", axis=0, tiled=True)
        partial = expert_part(rows, up_weight[expert], down_weight[expert])
        total = lax.psum_scatter(partial, "seq", scatter_dimension=0, tiled=True)
        total = total.reshape(exp_count, capacity, model_dim)
        summed.append(lax.all_to_all(total, "exp", split_axis=0, concat_axis=0, tiled=True))
    summed = jnp.stack(summed, axis=1).reshape(EXPERTS * capacity, model_dim)
    combined = jnp.dot(
        combiner.T, summed.astype(jnp.float32), precision=lax.Precision.HIGHEST
    )
    return (token_float + combined).astype(jnp.bfloat16)


def solution(mesh):
    return jax.shard_map(
        per_device,
        mesh=mesh,
        in_specs=(
            P("seq", "exp"),
            P("seq", "exp"),
            P("seq", "exp"),
            P("seq", "exp"),
            P("seq", "exp"),
            P("exp"),
            P(),
            P(("seq", "exp"), None),
            P(("seq", "exp"), None),
            P("exp", None, "seq"),
            P("exp", "seq", None),
        ),
        out_specs=P(("seq", "exp"), None),
        check_vma=False,
    )
```
